256 devices in a mesh: dp: 64 (over z, y_lo, x), tensor: 4 (over y_hi, core).
Axes of the slice: x: 4, y: 4 (y_hi: 2, y_lo: 2; y = y_hi * 2 + y_lo), z: 8, core: 2. Of those that a mesh axis runs over, the one named last changes fastest.
Arguments:
- activations: bfloat16 [8192, 4096], P('dp'), may hold values from -6 to 6
- grad_out: bfloat16 [8192, 14336], P('dp', 'tensor'), may hold values from -16 to 16
- weight_codes: int32 [4096, 14336], P('dp', 'tensor'), may hold values from 0 to 15
- scales: bfloat16 [32, 14336], P(None, 'tensor'), may hold values from 0.00049972534 to 0.0079956055
- zero_points: int32 [32, 14336], P(None, 'tensor'), may hold values from 0 to 15
Outputs:
- grad_inputs: bfloat16 [8192, 4096], P('dp', 'tensor')
- grad_log_scales: float32 [32, 4, 3584], P(None, 'tensor', 'dp')
- grad_zero_points: float32 [32, 4, 3584], P(None, 'tensor', 'dp')
The draws below stay inside these ranges and needn't reach their ends.
Inputs may be any that keep to these rules, and one draw needn't show every extreme that they name: `weight_codes`: codes of the 4-bit weight.
All inputs are finite; a program needn't handle non-finite values.
Results may differ from the reference program's by a relative error of at most 0.012.
Values may be sent and summed in bfloat16 or wider, within the bound.
A program may use at most 128 MiB of HBM per device.

```python
import math
import jax
import jax.numpy as jnp
from jax import lax

D = 4096
FF = 14336
GROUP = 128
G = 32
FFT = 3584
TOKENS = 8192
N_TENSOR = 4


def place_ends(drawn, stream_key, least, high):
    longest = drawn.shape.index(max(drawn.shape))
    spots = []
    for shift in (0, 1):
        where = [jax.random.randint(jax.random.fold_in(stream_key, axis), (), 0, length) for axis, length in enumerate(drawn.shape)]
        where[longest] = (where[longest] + shift) % drawn.shape[longest]
        spots.append(tuple(where))
    return drawn.at[spots[0]].set(least).at[spots[1]].set(high)


def spiked(result, key, source, target, blocks, factor):
    def block_of(axis_at):
        return (jnp.arange(result.shape[axis_at]) // (result.shape[axis_at] // blocks)).reshape((-1,) + (1,) * (result.ndim - 1 - axis_at))

    first = jax.random.permutation(key, blocks)[block_of(target)]
    second = (block_of(target) + blocks // 2) % blocks
    return jnp.where((block_of(source) == first) | (block_of(source) == second), factor * result, result)


def block_scale(stream_key, shape, shards, low, high):
    factor_of = 1.0
    for dim, shards_of in shards:
        draws = jax.random.uniform(jax.random.fold_in(jax.random.fold_in(stream_key, 6), dim), (shards_of,), jnp.float32, low / len(shards), high / len(shards))
        factor_of = factor_of * jnp.repeat(jnp.exp(draws), shape[dim] // shards_of).reshape((-1,) + (1,) * (len(shape) - 1 - dim))
    return factor_of


def centred(key, shape, spread, reach, split=(), kind=jnp.bfloat16):
    array = spread * jax.random.normal(key, shape, jnp.float32)
    if split:
        array = array * block_scale(key, shape, split, -0.22, 0.18)
    return jnp.clip(array, -reach, reach).astype(kind)


def noise_with(key, shape, width, most, cuts, heavy, held_as=jnp.bfloat16):
    entries = width * jax.random.normal(key, shape, jnp.float32)
    if cuts:
        entries = entries * block_scale(key, shape, cuts, -0.22, 0.18)
    return jnp.clip(spiked(entries, jax.random.fold_in(key, 3), *heavy), -most, most).astype(held_as)


def setup_inputs(seed: int = 0) -> dict:
    streams_of = jax.random.split(jax.random.key(seed), 6)
    activations = centred(streams_of[0], (TOKENS, D), 1.0, 6.0, ((0, 64),))
    grad_out = noise_with(streams_of[1], (TOKENS, FF), 1.0, 16.0, ((0, 64), (1, 4)), (0, 1, 64, 4.0))
    weight_codes = place_ends(jax.random.randint(streams_of[2], (D, FF), 0, 16), jax.random.fold_in(streams_of[2], 1), 0, 15).astype(jnp.int32)
    scales = jnp.clip(jnp.exp(math.log(0.0079956055) - 2.7725887 * jax.random.uniform(streams_of[3], (G, FF), jnp.float32) ** block_scale(streams_of[3], (G, FF), ((1, 4),), -0.2, 0.2)), 0.00049972534, 0.0079956055).astype(jnp.bfloat16)
    zero_points = place_ends(jax.random.randint(streams_of[4], (G, FF), 0, 16), jax.random.fold_in(streams_of[4], 1), 0, 15).astype(jnp.int32)
    return dict(activations=activations, grad_out=grad_out, weight_codes=weight_codes, scales=scales, zero_points=zero_points)


def reference(activations, grad_out, weight_codes, scales, zero_points):
    groups = D // GROUP

    def tensor_block(running, index):
        first_col = (index * FFT).astype(jnp.int32)
        grad_cols = lax.dynamic_slice_in_dim(grad_out, first_col, FFT, 1)
        code_cols = lax.dynamic_slice_in_dim(weight_codes, first_col, FFT, 1)
        scale_cols = lax.dynamic_slice_in_dim(scales, first_col, FFT, 1).astype(jnp.float32)
        zero_cols = lax.dynamic_slice_in_dim(zero_points, first_col, FFT, 1).astype(jnp.float32)
        scale_rows = jnp.repeat(scale_cols, GROUP, axis=0)
        zero_rows = jnp.repeat(zero_cols, GROUP, axis=0)
        weight = (scale_rows * (code_cols.astype(jnp.float32) - zero_rows)).astype(jnp.bfloat16)
        term = lax.dot_general(grad_cols, weight, (((1,), (1,)), ((), ())), preferred_element_type=jnp.float32)
        term = lax.optimization_barrier(term.astype(jnp.bfloat16)).astype(jnp.float32)
        running = running + term
        grad_weight = lax.dot_general(activations, grad_cols, (((0,), (0,)), ((), ())), preferred_element_type=jnp.float32)
        log_terms = (grad_weight * weight.astype(jnp.float32)).reshape(groups, GROUP, FFT).sum(axis=1)
        sum_terms = grad_weight.reshape(groups, GROUP, FFT).sum(axis=1)
        return running, (log_terms, -scale_cols * sum_terms)

    running = jnp.zeros((TOKENS, D), jnp.float32)
    running, (log_terms, zero_terms) = lax.scan(tensor_block, running, jnp.arange(N_TENSOR, dtype=jnp.int32))
    return (running.astype(jnp.bfloat16), jnp.transpose(log_terms, (1, 0, 2)), jnp.transpose(zero_terms, (1, 0, 2)))
```

```python
import jax
import jax.numpy as jnp
from jax import lax
from jax.sharding import Mesh, PartitionSpec as P

GROUP = 128
NZ, NL, NX, NH, NK = 8, 2, 4, 2, 2


def dequantize(weight_codes, scales, zero_points, dp):
    rows = weight_codes.shape[0]
    group = dp * rows // GROUP
    scale_row = lax.dynamic_slice_in_dim(scales, group, 1, 0).astype(jnp.float32)
    zero_row = lax.dynamic_slice_in_dim(zero_points, group, 1, 0)
    return (scale_row * (weight_codes - zero_row).astype(jnp.float32)).astype(jnp.bfloat16)


def on_device(activations, grad_out, weight_codes, scales, zero_points):
    iz, il, ix = lax.axis_index("z"), lax.axis_index("l"), lax.axis_index("x")
    dp = (iz * NL + il) * NX + ix
    tokens, features = activations.shape
    rows, cols = weight_codes.shape
    half = cols // NL
    groups = scales.shape[0]
    weight = dequantize(weight_codes, scales, zero_points, dp)
    w = lax.all_to_all(weight.reshape(rows, NL, half), "l", 1, 0, tiled=False)
    go = lax.all_to_all(grad_out.reshape(tokens, NL, half), "l", 1, 0, tiled=False)
    w = w.reshape(NL * rows, half)
    go = go.reshape(NL * tokens, half)
    w = lax.all_gather(w, "z", axis=0, tiled=True)
    go = lax.all_gather(go, "x", axis=0, tiled=True)
    act = activations.reshape(tokens, NZ * NL, NX, rows)
    act = lax.all_to_all(act, "x", 2, 0, tiled=False)
    act = lax.all_gather(act, "l", axis=1, tiled=False)
    act = act.reshape(NX * NL * tokens, NZ * NL * rows)

    out = lax.dot_general(go, w, (((1,), (1,)), ((), ())), preferred_element_type=jnp.float32)
    out = out.astype(jnp.bfloat16).reshape(NX, NL, tokens, NH * NK, 2 * NL * rows)
    out = jnp.transpose(out, (1, 3, 0, 2, 4))
    out = out.reshape(NL * NH * NK, NX, tokens, 2 * NL * rows)
    out = lax.psum_scatter(out, ("l", "h", "k"), scatter_dimension=0, tiled=True)[0]
    out = lax.all_to_all(out, "x", 0, 0, tiled=False)
    out = out.reshape(NX, tokens, 2 * NL, rows)
    feature_grad = jnp.transpose(out, (1, 2, 0, 3)).reshape(tokens, features // 4)

    gw = lax.dot_general(act, go, (((0,), (0,)), ((), ())), preferred_element_type=jnp.float32)
    log_part = (gw * w.astype(jnp.float32)).reshape(NZ * NL, rows, half).sum(axis=1)
    sum_part = gw.reshape(NZ * NL, rows, half).sum(axis=1)
    parts = jnp.stack([log_part, sum_part]).reshape(2, NZ, NL, half)
    parts = lax.all_to_all(parts, "z", 1, 0, tiled=False).sum(axis=0)
    width = cols // (NZ * NL * NX)
    dests = half // width
    parts = jnp.transpose(parts.reshape(2, NL, dests, width), (2, 0, 1, 3))
    full = jnp.zeros((NL * dests, 2, NL, width), jnp.float32)
    full = lax.dynamic_update_slice(full, parts, (il * dests, 0, 0, 0))
    share = lax.all_to_all(full, ("z", "l", "x"), 0, 0, tiled=True)
    share = share.reshape(NZ, NL, NX // 2, 2, 2, NL, width).sum(axis=(1, 3))
    share = jnp.transpose(share, (2, 0, 3, 1, 4)).reshape(2, groups, width)
    scale_share = lax.dynamic_slice_in_dim(scales, dp * width, width, 1).astype(jnp.float32)
    return (feature_grad, share[0][:, None, :], (-scale_share * share[1])[:, None, :])


def solution(mesh):
    fine = Mesh(mesh.devices.reshape(NZ, NL, NX, NH, NK), ("z", "l", "x", "h", "k"))
    dp, tensor = ("z", "l", "x"), ("h", "k")
    in_specs = (P(dp, None), P(dp, tensor), P(dp, tensor), P(None, tensor), P(None, tensor))
    out_specs = (P(dp, tensor), P(None, tensor, dp), P(None, tensor, dp))
    return jax.shard_map(
        on_device, mesh=fine, in_specs=in_specs, out_specs=out_specs, check_vma=False
    )
```

```python
import jax
import jax.numpy as jnp
from jax import lax
from jax.experimental import pallas as pl
from jax.experimental.pallas import tpu as pltpu
from jax.sharding import PartitionSpec as P

NZ, NL, NX, NH, NK = 8, 2, 4, 2, 2
MESH = pl.DeviceIdType.MESH
F32, BF16 = jnp.float32, jnp.bfloat16
Z_OFF = (0, 1, 7, 2, 6, 3, 5, 4)
Z_INV = (0, 2, 1, 4, 3, 6, 5, 7)
X_OFF = (0, 1, 3, 2)
X_INV = (0, 2, 1, 3)


def kernel(
    act_ref, go_ref, codes_ref, scales_ref, zeros_ref,
    out_ref, log_ref, zero_ref,
    act_v, codes_v, scales_v, zeros_v, scale32, fsend, frecv, wbuf, wsend, gbuf, act_t, asend, abuf, obuf, krecv, ybuf, yrecv, yown, xrecv,
    fin, lacc, lsent, lrecv,
    ins, zs, zr, xs, xr, ys, yr, as_, ar, ks, kr, os_, or_, fs, fr, ls, lr, es, er,
):
    dp, tensor = lax.axis_index("dp"), lax.axis_index("tensor")
    z, l, x = dp // (NL * NX), (dp // NX) % NL, dp % NX
    h, k = tensor // NK, tensor % NK
    rows, cols = codes_ref.shape
    tokens = go_ref.shape[0]
    half = cols // NL
    chunk = NL * rows
    nt = NX * tokens
    quarter = lacc.shape[2]

    def at(z_=z, l_=l, x_=x, h_=h, k_=k):
        return ((z_ * NL + l_) * NX + x_, h_ * NK + k_)

    direct = at(l_=1 - l)
    wrap = at(l_=1 - l, h_=1 - h)
    across = at(h_=1 - h)
    core = at(k_=1 - k)
    xs_of = [at(x_=(x + o) % NX) for o in X_OFF]
    zs_of = [at(z_=(z + o) % NZ) for o in Z_OFF]

    def copy(src, dst, send, recv, device):
        return pltpu.make_async_remote_copy(
            src_ref=src, dst_ref=dst, send_sem=send, recv_sem=recv,
            device_id=device, device_id_type=MESH,
        )

    def send(src, dst, s, r, device):
        copy(src, dst, s, r, device).start()

    def all_sent(ref, s):
        copy(ref, ref, s, s, core).wait_send()

    def arrived(dst, s, r):
        copy(dst, dst, s, r, core).wait_recv()

    own_cols = pl.ds(pl.multiple_of(l * half, 128), half)
    other_cols = pl.ds(pl.multiple_of((1 - l) * half, 128), half)
    group = dp // 2
    base = pl.multiple_of(group // 16 * 16, 16)
    barrier = pltpu.get_barrier_semaphore()
    loads = [
        pltpu.make_async_copy(src, dst, ins.at[i])
        for i, (src, dst) in enumerate((
            (scales_ref.at[pl.ds(base, 16), :], scales_v),
            (zeros_ref.at[pl.ds(base, 16), :], zeros_v),
            (codes_ref.at[:, other_cols], codes_v.at[1]),
            (codes_ref.at[:, own_cols], codes_v.at[0]),
            (act_ref, act_v),
            (go_ref.at[:, own_cols], gbuf.at[0:tokens, :]),
        ))
    ]
    for load in loads:
        load.start()
    partners = zs_of[1:3] + xs_of[1:] + [direct, wrap, core]
    for device in partners:
        pl.semaphore_signal(barrier, inc=1, device_id=device, device_id_type=MESH)
    lows = NZ // NL
    is_mine = z // lows == l
    part_rows = (
        pl.multiple_of(l * rows, rows),
        pl.multiple_of((1 - l) * rows, rows),
    )
    loads[0].wait()
    loads[1].wait()
    scale32[...] = scales_v[...].astype(F32)

    def dequantized(side, columns):
        scale = scale32[pl.ds(group - base, 1), columns]
        zero = zeros_v[pl.ds(group - base, 1), columns]
        return (scale * (codes_v[side] - zero).astype(F32)).astype(BF16)

    loads[2].wait()
    wsend[...] = dequantized(1, other_cols)
    loads[3].wait()
    wbuf[pl.ds(part_rows[0], rows), :] = dequantized(0, own_cols)
    features = act_ref.shape[1]
    loads[4].wait()
    for c in range(0, features, 128):
        act_t[c:c + 128, :] = act_v[:, c:c + 128].T
    hrows = NZ // 2 * chunk
    my_half = pl.multiple_of(k * hrows, hrows)
    for i in range(NZ // 2):
        z_at = (z + jnp.where(k == 0, Z_OFF[i], Z_OFF[NZ // 2 + i])) % NZ
        for l_at in range(NL):
            for j in range(NX):
                first = pl.multiple_of(((z_at * NL + l_at) * NX + (x + X_OFF[j]) % NX) * rows, rows)
                piece = act_t[pl.ds(first, rows), :]
                place = i * chunk + l_at * rows
                if j:
                    asend[j - 1, place:place + rows, :] = piece
                else:
                    abuf[pl.ds(pl.multiple_of(my_half + place, rows), rows), 0:tokens] = piece

    pl.semaphore_wait(barrier, len(partners))

    def wrows(slot, part, sub=None):
        count = rows if sub is None else rows // 2
        return wbuf.at[pl.ds(slot * chunk + part_rows[part] + (sub or 0) * (rows // 2), count), :]

    def zcopy(step, part, sub, way):
        src = wrows(2 * step - way if step else 0, part, sub)
        dst = wrows(2 * (step + 1) - way if step < 3 else 7, part, sub)
        i = ((way * 4 + step) * 2 + part) * 2 + sub
        return src, dst, zs.at[0], zr.at[i], zs_of[1 + way]

    def zpass(step, part):
        for n in range(2):
            for way in range(2):
                sub = n if way == 0 else 1 - n
                if step:
                    arrived(*zcopy(step - 1, part, sub, way)[1:4])
                if step < 3 or n == 0:
                    send(*zcopy(step, part, sub, way))

    def zlast(part):
        for way in range(2):
            arrived(*zcopy(3, part, way, way)[1:4])

    def grows(slot, part, first=0, count=None):
        start = part * nt + slot * tokens + first
        return gbuf.at[start:start + (count or tokens), :]

    turn = tokens * 3 // 8

    def xcopy(kind, part, way):
        first, count = (0, turn) if (kind == 1) == (way == 1) else (turn, tokens - turn)
        if kind == 2:
            src, dst = grows(2 - way, part, first, count), grows(3, part, first, count)
        else:
            src = grows(0, 1, first, count) if part else go_ref.at[first:first + count, own_cols]
            dst = grows(2 - way, part, first, count)
        i = (way * 3 + kind) * 2 + part
        return src, dst, xs.at[0], xr.at[i], xs_of[1 + way]

    def xown(part):
        for kind in (0, 1):
            for way in range(2):
                send(*xcopy(kind, part, way))

    def xpass(part):
        for way in range(2):
            arrived(*xcopy(0, part, way)[1:4])
            send(*xcopy(2, part, way))

    def xwait(kind, part):
        for way in range(2):
            arrived(*xcopy(kind, part, way)[1:4])

    def ablock(first, count, half_at=None):
        start = my_half if half_at is None else half_at
        return abuf.at[pl.ds(start, hrows), first:first + count]

    send(wsend, wrows(0, 0), ys.at[0], yr.at[0], direct)
    zpass(0, 0)
    for j in range(1, NX):
        send(asend.at[j - 1], ablock(X_INV[j] * tokens, tokens), as_.at[0], ar.at[X_INV[j] - 1], xs_of[j])
    xown(0)

    lacc[...] = jnp.zeros_like(lacc)

    def mix(r0, nr, t0, n):
        r, t = slice(r0, r0 + nr), slice(t0, t0 + n)
        obuf[r, t] = lax.dot_general(
            wbuf[r, :], gbuf[t, :], (((1,), (1,)), ((), ())), preferred_element_type=F32
        ).astype(BF16)

    def sums(r0, nr, t0, n):
        r, t = slice(r0, r0 + nr), slice(t0, t0 + n)
        for cc in range(2):
            c = slice(cc * quarter, (cc + 1) * quarter)
            gw = jnp.dot(abuf[r, t], gbuf[t, c], preferred_element_type=F32)
            for piece in range(nr // rows):
                p = slice(piece * rows, (piece + 1) * rows)
                g = gw[p]
                w = wbuf[r0 + piece * rows:r0 + (piece + 1) * rows, c].astype(F32)
                slot, l_at = (r0 // rows + piece) // NL, piece % NL
                at_row = cc * 4 + l_at
                lacc[slot, at_row:at_row + 1, :] += jnp.sum(g * w, axis=0, keepdims=True)
                lacc[slot, at_row + 2:at_row + 3, :] += jnp.sum(g, axis=0, keepdims=True)

    def compute(r0, nr, t0, n):
        mix(r0, nr, t0, n)
        sums(r0, nr, t0, n)

    def z_at(slot):
        return (z + Z_OFF[slot]) % NZ

    early = (NX - 1) * tokens
    lanes = (slice(0, nt), slice(nt, nt + early), slice(nt + early, 2 * nt))
    into = (slice(0, nt), slice(0, early), slice(early, nt))

    def tile(buf, slot, part):
        return buf.at[slot * chunk:(slot + 1) * chunk, lanes[part]]

    def slot_of(z_to):
        off = (z_to - z + NZ) % NZ
        return jnp.where(off == 0, 0, jnp.where(off < 4, 2 * off - 1, jnp.where(off == 4, 7, 2 * (NZ - off))))

    def ycopy(src, dst_at, part, zp, device):
        dst = yrecv.at[dst_at, zp, :, into[part]]
        return copy(src, dst, os_.at[0], or_.at[(dst_at * 3 + part) * 2 + zp], device)

    def block(buf, slot):
        return buf.at[pl.ds(pl.multiple_of(slot * chunk, chunk), chunk), lanes[2]]

    def last_send():
        for n in range(4):
            slot = slot_of(n // 2 * 4 + 2 * (1 - k) + n % 2)
            copy(block(obuf, slot), block(krecv, slot), ks.at[0], kr.at[slot * 3 + 2], core).start()

    def last_drain():
        for n in range(4):
            slot = slot_of(n // 2 * 4 + 2 * k + n % 2)
            arrived(block(krecv, slot), ks.at[0], kr.at[slot * 3 + 2])
            total = block(obuf, slot)[...].astype(F32) + block(krecv, slot)[...].astype(F32)
            block(ybuf, slot)[...] = total.astype(BF16)
            ycopy(block(ybuf, slot), jnp.where(h == n // 2, 1, 2), 2, n % 2, at(l_=1 - l, h_=n // 2)).start()

    def ksend(slots, parts):
        for slot in slots:
            for part in parts:
                i = slot * 3 + part

                @pl.when((z_at(slot) // 2) % 2 != k)
                def _():
                    copy(tile(obuf, slot, part), tile(krecv, slot, part), ks.at[0], kr.at[i], core).start()

    def kdrain_one(slot, part):
        i = slot * 3 + part
        zz = z_at(slot)

        @pl.when((zz // 2) % 2 == k)
        def _():
            arrived(tile(krecv, slot, part), ks.at[0], kr.at[i])
            total = tile(obuf, slot, part)[...].astype(F32) + tile(krecv, slot, part)[...].astype(F32)
            tile(ybuf, slot, part)[...] = total.astype(BF16)
            zp = zz % 2
            src = tile(ybuf, slot, part)
            if part == 0:
                @pl.when(zz // 4 != h)
                def _():
                    ycopy(src, 0, part, zp, across).start()
            else:
                ycopy(src, jnp.where(zz // 4 == h, 1, 2), part, zp, at(l_=1 - l, h_=zz // 4)).start()

    def kdrain(slots, parts):
        for slot in slots:
            for part in parts:
                kdrain_one(slot, part)

    eighth = quarter // 2

    def folded(slot):
        return jnp.concatenate([lacc[slot, :, 0:eighth], lacc[slot, :, eighth:quarter]], axis=0)

    def lsend(slot):
        lsent[slot - 1, :, 0:eighth] = folded(slot).astype(BF16)
        send(lsent.at[slot - 1], lrecv.at[Z_INV[slot] - 1], ls.at[0], lr.at[Z_INV[slot] - 1], zs_of[slot])

    t1, t2, t3, t4 = 3 * tokens, 2 * tokens, 2 * tokens, tokens
    zpass(1, 0)
    send(go_ref.at[:, other_cols], grows(0, 1), ys.at[0], yr.at[1], direct)
    arrived(wrows(0, 1), ys.at[0], yr.at[0])
    zpass(0, 1)
    for j in range(1, NX):
        arrived(ablock(j * tokens, tokens), as_.at[0], ar.at[j - 1])
    send(ablock(0, nt), ablock(0, nt), as_.at[0], ar.at[3], core)
    send(ablock(0, nt), ablock(nt, nt), as_.at[0], ar.at[4], wrap)
    zpass(2, 0)
    xpass(0)
    zpass(1, 1)
    loads[5].wait()
    arrived(grows(0, 1), ys.at[0], yr.at[1])
    xown(1)
    xwait(1, 0)
    other_half = pl.multiple_of((1 - k) * hrows, hrows)
    arrived(ablock(0, nt, other_half), as_.at[0], ar.at[3])
    compute(0, 3 * chunk, 0, t1)
    zpass(3, 0)
    arrived(ablock(nt, nt), as_.at[0], ar.at[4])
    send(ablock(nt, nt), ablock(nt, nt), as_.at[0], ar.at[5], core)
    zpass(2, 1)
    xwait(2, 0)
    arrived(ablock(nt, nt, other_half), as_.at[0], ar.at[5])
    compute(0, 3 * chunk, t1, t2)
    ksend((0, 1, 2), (0,))
    xpass(1)
    compute(3 * chunk, 2 * chunk, 0, t1 + t2)
    ksend((3, 4), (0,))
    kdrain((0, 1, 2), (0,))
    zpass(3, 1)
    xwait(1, 1)
    compute(0, 5 * chunk, t1 + t2, t3)
    ksend((0, 1, 2, 3, 4), (1,))
    kdrain((3, 4), (0,))
    compute(5 * chunk, 2 * chunk, 0, t1 + t2 + t3)
    ksend((5, 6), (0, 1))
    kdrain((0, 1, 2, 3, 4), (1,))
    xwait(2, 1)
    mix(0, 7 * chunk, t1 + t2 + t3, t4)
    kdrain((5, 6), (0, 1))
    zlast(0)
    zlast(1)
    mix(7 * chunk, chunk, 0, 2 * nt)
    ksend((7,), (0, 1))
    last_send()
    sums(0, 7 * chunk, t1 + t2 + t3, t4)
    for s in range(1, 7):
        lsend(s)
    kdrain((7,), (0, 1))
    last_drain()
    sums(7 * chunk, chunk, 0, 2 * nt)
    lsend(7)

    total = folded(0)
    for s in range(1, NZ):
        arrived(lrecv.at[s - 1], ls.at[0], lr.at[s - 1])
        total += lrecv[s - 1, :, 0:eighth].astype(F32)
    factors = []
    for side in range(2):
        for cc in range(2):
            columns = pl.ds(pl.multiple_of(l * half + cc * quarter, 128), quarter)
            factors.append(jnp.ones((2, eighth), F32))
            for l_at in range(NL):
                scale = scale32[pl.ds((z * NL + l_at) * 2 + x // 2 - base, 1), columns]
                factors.append(-scale[:, side * eighth:(side + 1) * eighth])
    total *= jnp.concatenate(factors, axis=0)
    width = log_ref.shape[1]
    for j in range(fsend.shape[0]):
        cc, m = j // (quarter // width), j % (quarter // width)
        side, m = m // (eighth // width), m % (eighth // width)
        fsend[j, :, 0:width] = total[side * 8 + cc * 4:side * 8 + cc * 4 + 4, m * width:(m + 1) * width]
    here = z * NX + x
    for n in range(lows * NL * NX):
        zq, l_to, x_to = (z + n // (NL * NX)) % lows, (l + n // NX) % NL, (x + n) % NX
        src, dst = fsend.at[(zq * NL + l_to) * NX + x_to], frecv.at[here]
        device = at(z_=l * lows + zq, l_=l_to, x_=x_to)
        if n:
            copy(src, dst, es.at[0], er.at[0], device).start()
        else:
            @pl.when(jnp.logical_not(is_mine))
            def _():
                copy(src, dst, es.at[0], er.at[0], device).start()

            @pl.when(is_mine)
            def _():
                pltpu.make_async_copy(src, dst, er.at[0]).start()

    q = h * NK + k
    for part in (1, 2):
        for zp in range(2):
            slot = slot_of(2 * q + zp)
            if part == 1:
                arrived(yrecv.at[0, zp], os_.at[0], or_.at[zp])
            for src in (1, 2):
                arrived(yrecv.at[src, zp, :, into[part]], os_.at[0], or_.at[(src * 3 + part) * 2 + zp])
            total = ybuf[pl.ds(pl.multiple_of(slot * chunk, chunk), chunk), into[part]].astype(F32)
            for src in range(3):
                total += yrecv[src, zp, :, into[part]].astype(F32)
            yown[zp, :, into[part]] = total.astype(BF16)
            for j in (1, 2) if part == 1 else (3,):
                i = (j - 1) * 2 + zp
                r = (X_INV[j] - 1) * 2 + zp
                send(yown.at[zp, :, j * tokens:(j + 1) * tokens], xrecv.at[X_INV[j] - 1, zp], fs.at[0], fr.at[r], xs_of[j])

    for zp in range(2):
        for j in range(NX):
            if j:
                arrived(xrecv.at[j - 1, zp], fs.at[0], fr.at[(j - 1) * 2 + zp])
            x_at = (x + X_OFF[j]) % NX
            for l_at in range(NL):
                p = slice(l_at * rows, (l_at + 1) * rows)
                piece = xrecv[j - 1, zp, p, :] if j else yown[zp, p, 0:tokens]
                first = ((zp * NL + l_at) * NX + x_at) * rows
                fin[pl.ds(pl.multiple_of(first, rows), rows), :] = piece
    for c in range(0, fin.shape[0], 128):
        out_ref[:, c:c + 128] = fin[c:c + 128, :].T

    copy(frecv, frecv, es.at[0], er.at[0], core).wait_recv()
    for zj in range(NZ):
        for pair in range(NX // 2):
            four = frecv[zj * NX + 2 * pair] + frecv[zj * NX + 2 * pair + 1]
            for l_at in range(NL):
                g = (zj * NL + l_at) * 2 + pair
                log_ref[g:g + 1, :] = four[l_at:l_at + 1, 0:width]
                zero_ref[g:g + 1, :] = four[2 + l_at:3 + l_at, 0:width]

    all_sent(wbuf.at[0:7 * chunk, :], zs.at[0])
    all_sent(gbuf.at[0:6 * tokens, :], xs.at[0])
    all_sent(wsend, ys.at[0])
    all_sent(grows(0, 0), ys.at[0])
    all_sent(asend, as_.at[0])
    for _ in range(3):
        all_sent(ablock(0, nt), as_.at[0])
    all_sent(obuf.at[0:4 * chunk, :], ks.at[0])
    all_sent(ybuf.at[0:3 * chunk, :], os_.at[0])
    all_sent(xrecv, fs.at[0])
    all_sent(lsent, ls.at[0])
    copy(frecv.at[0:NZ * NX - 1], frecv.at[0:NZ * NX - 1], es.at[0], er.at[0], core).wait_send()

    @pl.when(jnp.logical_not(is_mine))
    def _():
        copy(frecv.at[0], frecv.at[0], es.at[0], er.at[0], core).wait_send()


def on_device(activations, grad_out, weight_codes, scales, zero_points):
    tokens, features = activations.shape
    rows, cols = weight_codes.shape
    half = cols // NL
    groups = scales.shape[0]
    chunk, nt = NL * rows, NX * tokens
    vmem = pl.BlockSpec(memory_space=pltpu.VMEM)
    dma = pltpu.SemaphoreType.DMA
    width = cols // (NZ * NL * NX)
    hbm = pl.BlockSpec(memory_space=pltpu.HBM)
    out, log_sums, zero_sums = pl.pallas_call(
        kernel,
        out_shape=(
            jax.ShapeDtypeStruct((tokens, features // (NH * NK)), BF16),
            jax.ShapeDtypeStruct((groups, width), F32),
            jax.ShapeDtypeStruct((groups, width), F32),
        ),
        in_specs=[hbm] * 5,
        out_specs=(vmem, vmem, vmem),
        scratch_shapes=[
            pltpu.VMEM((tokens, features), BF16),
            pltpu.VMEM((2, rows, half), jnp.int32),
            pltpu.VMEM((16, cols), BF16),
            pltpu.VMEM((16, cols), jnp.int32),
            pltpu.VMEM((16, cols), F32),
            pltpu.VMEM((half // width, 4, 128), F32),
            pltpu.VMEM((NZ * NX, 4, 128), F32),
            pltpu.VMEM((NZ * chunk, half), BF16),
            pltpu.VMEM((rows, half), BF16),
            pltpu.VMEM((NL * nt, half), BF16),
            pltpu.VMEM((features, tokens), BF16),
            pltpu.VMEM((NX - 1, NZ // 2 * chunk, tokens), BF16),
            pltpu.VMEM((NZ * chunk, NL * nt), BF16),
            pltpu.VMEM((NZ * chunk, NL * nt), BF16),
            pltpu.VMEM((NZ * chunk, NL * nt), BF16),
            pltpu.VMEM((NZ * chunk, NL * nt), BF16),
            pltpu.VMEM((3, 2, chunk, nt), BF16),
            pltpu.VMEM((2, chunk, nt), BF16),
            pltpu.VMEM((NX - 1, 2, chunk, tokens), BF16),
            pltpu.VMEM((2 * NX * chunk, tokens), BF16),
            pltpu.VMEM((NZ, 8, half // 2), F32),
            pltpu.VMEM((NZ - 1, 16, 512), BF16),
            pltpu.VMEM((NZ - 1, 16, 512), BF16),
            dma((6,)),
            dma((1,)), dma((32,)),
            dma((1,)), dma((12,)),
            dma((1,)), dma((2,)),
            dma((1,)), dma((6,)),
            dma((1,)), dma((24,)),
            dma((1,)), dma((18,)),
            dma((1,)), dma((6,)),
            dma((1,)), dma((7,)),
            dma((1,)), dma((1,)),
        ],
        compiler_params=pltpu.CompilerParams(
            collective_id=0, has_side_effects=True, vmem_limit_bytes=63 * 2**20
        ),
        cost_estimate=pl.CostEstimate(
            flops=4 * NZ * chunk * NL * nt * half, bytes_accessed=4 * 2**20, transcendentals=0
        ),
    )(activations, grad_out, weight_codes, scales, zero_points)

    return (out, log_sums[:, None, :], zero_sums[:, None, :])


def solution(mesh):
    in_specs = (
        P("dp", None),
        P("dp", "tensor"),
        P("dp", "tensor"),
        P(None, "tensor"),
        P(None, "tensor"),
    )
    out_specs = (P("dp", "tensor"), P(None, "tensor", "dp"), P(None, "tensor", "dp"))
    return jax.shard_map(
        on_device, mesh=mesh, in_specs=in_specs, out_specs=out_specs, check_vma=False
    )
```

```python
import jax
import jax.numpy as jnp
from jax import lax
from jax.experimental import pallas as pl
from jax.experimental.pallas import tpu as pltpu
from jax.sharding import PartitionSpec as P

NZ, NL, NX, NH, NK = 8, 2, 4, 2, 2
MESH = pl.DeviceIdType.MESH
F32, BF16 = jnp.float32, jnp.bfloat16
Z_OFF = (0, 1, 7, 2, 6, 3, 5, 4)
Z_INV = (0, 2, 1, 4, 3, 6, 5, 7)
X_OFF = (0, 1, 3, 2)
X_INV = (0, 2, 1, 3)


def kernel(
    act_ref, go_ref, codes_ref, scales_ref, zeros_ref,
    out_ref, log_ref, zero_ref,
    act_v, codes_v, scales_v, zeros_v, scale32, fsend, frecv, wbuf, wsend, gbuf, act_t, asend, abuf, obuf, krecv, ybuf, yrecv, yown, xrecv,
    fin, lacc, lsent, lrecv,
    ins, zs, zr, xs, xr, ys, yr, as_, ar, ks, kr, os_, or_, fs, fr, ls, lr, es, er,
):
    dp, tensor = lax.axis_index("dp"), lax.axis_index("tensor")
    z, l, x = dp // (NL * NX), (dp // NX) % NL, dp % NX
    h, k = tensor // NK, tensor % NK
    rows, cols = codes_ref.shape
    tokens = go_ref.shape[0]
    half = cols // NL
    chunk = NL * rows
    nt = NX * tokens
    quarter = lacc.shape[2]

    def at(z_=z, l_=l, x_=x, h_=h, k_=k):
        return ((z_ * NL + l_) * NX + x_, h_ * NK + k_)

    direct = at(l_=1 - l)
    wrap = at(l_=1 - l, h_=1 - h)
    across = at(h_=1 - h)
    core = at(k_=1 - k)
    xs_of = [at(x_=(x + o) % NX) for o in X_OFF]
    zs_of = [at(z_=(z + o) % NZ) for o in Z_OFF]

    def copy(src, dst, send, recv, device):
        return pltpu.make_async_remote_copy(
            src_ref=src, dst_ref=dst, send_sem=send, recv_sem=recv,
            device_id=device, device_id_type=MESH,
        )

    def send(src, dst, s, r, device):
        copy(src, dst, s, r, device).start()

    def all_sent(ref, s):
        copy(ref, ref, s, s, core).wait_send()

    def arrived(dst, s, r):
        copy(dst, dst, s, r, core).wait_recv()

    own_cols = pl.ds(pl.multiple_of(l * half, 128), half)
    other_cols = pl.ds(pl.multiple_of((1 - l) * half, 128), half)
    group = dp // 2
    base = pl.multiple_of(group // 16 * 16, 16)
    barrier = pltpu.get_barrier_semaphore()
    loads = [
        pltpu.make_async_copy(src, dst, ins.at[i])
        for i, (src, dst) in enumerate((
            (scales_ref.at[pl.ds(base, 16), :], scales_v),
            (zeros_ref.at[pl.ds(base, 16), :], zeros_v),
            (codes_ref.at[:, other_cols], codes_v.at[1]),
            (codes_ref.at[:, own_cols], codes_v.at[0]),
            (act_ref, act_v),
            (go_ref.at[:, own_cols], gbuf.at[0:tokens, :]),
        ))
    ]
    for load in loads:
        load.start()
    partners = zs_of[1:3] + xs_of[1:] + [direct, wrap, core]
    for device in partners:
        pl.semaphore_signal(barrier, inc=1, device_id=device, device_id_type=MESH)
    lows = NZ // NL
    is_mine = z // lows == l
    part_rows = (
        pl.multiple_of(l * rows, rows),
        pl.multiple_of((1 - l) * rows, rows),
    )
    loads[0].wait()
    loads[1].wait()
    scale32[...] = scales_v[...].astype(F32)

    def dequantized(side, columns):
        scale = scale32[pl.ds(group - base, 1), columns]
        zero = zeros_v[pl.ds(group - base, 1), columns]
        return (scale * (codes_v[side] - zero).astype(F32)).astype(BF16)

    loads[2].wait()
    wsend[...] = dequantized(1, other_cols)
    loads[3].wait()
    wbuf[pl.ds(part_rows[0], rows), :] = dequantized(0, own_cols)
    features = act_ref.shape[1]
    loads[4].wait()
    for c in range(0, features, 128):
        act_t[c:c + 128, :] = act_v[:, c:c + 128].T
    hrows = NZ // 2 * chunk
    my_half = pl.multiple_of(k * hrows, hrows)
    for i in range(NZ // 2):
        z_at = (z + jnp.where(k == 0, Z_OFF[i], Z_OFF[NZ // 2 + i])) % NZ
        for l_at in range(NL):
            for j in range(NX):
                first = pl.multiple_of(((z_at * NL + l_at) * NX + (x + X_OFF[j]) % NX) * rows, rows)
                piece = act_t[pl.ds(first, rows), :]
                place = i * chunk + l_at * rows
                if j:
                    asend[j - 1, place:place + rows, :] = piece
                else:
                    abuf[pl.ds(pl.multiple_of(my_half + place, rows), rows), 0:tokens] = piece

    pl.semaphore_wait(barrier, len(partners))

    def wrows(slot, part, sub=None):
        count = rows if sub is None else rows // 2
        return wbuf.at[pl.ds(slot * chunk + part_rows[part] + (sub or 0) * (rows // 2), count), :]

    def zcopy(step, part, sub, way):
        src = wrows(2 * step - way if step else 0, part, sub)
        dst = wrows(2 * (step + 1) - way if step < 3 else 7, part, sub)
        i = ((way * 4 + step) * 2 + part) * 2 + sub
        return src, dst, zs.at[0], zr.at[i], zs_of[1 + way]

    def zpass(step, part):
        for n in range(2):
            for way in range(2):
                sub = n if way == 0 else 1 - n
                if step:
                    arrived(*zcopy(step - 1, part, sub, way)[1:4])
                if step < 3 or n == 0:
                    send(*zcopy(step, part, sub, way))

    def zlast(part):
        for way in range(2):
            arrived(*zcopy(3, part, way, way)[1:4])

    def grows(slot, part, first=0, count=None):
        start = part * nt + slot * tokens + first
        return gbuf.at[start:start + (count or tokens), :]

    turn = tokens * 3 // 8

    def xcopy(kind, part, way):
        first, count = (0, turn) if (kind == 1) == (way == 1) else (turn, tokens - turn)
        if kind == 2:
            src, dst = grows(2 - way, part, first, count), grows(3, part, first, count)
        else:
            src = grows(0, 1, first, count) if part else go_ref.at[first:first + count, own_cols]
            dst = grows(2 - way, part, first, count)
        i = (way * 3 + kind) * 2 + part
        return src, dst, xs.at[0], xr.at[i], xs_of[1 + way]

    def xown(part):
        for kind in (0, 1):
            for way in range(2):
                send(*xcopy(kind, part, way))

    def xpass(part):
        for way in range(2):
            arrived(*xcopy(0, part, way)[1:4])
            send(*xcopy(2, part, way))

    def xwait(kind, part):
        for way in range(2):
            arrived(*xcopy(kind, part, way)[1:4])

    def ablock(first, count, half_at=None):
        start = my_half if half_at is None else half_at
        return abuf.at[pl.ds(start, hrows), first:first + count]

    send(wsend, wrows(0, 0), ys.at[0], yr.at[0], direct)
    zpass(0, 0)
    for j in range(1, NX):
        send(asend.at[j - 1], ablock(X_INV[j] * tokens, tokens), as_.at[0], ar.at[X_INV[j] - 1], xs_of[j])
    xown(0)

    lacc[...] = jnp.zeros_like(lacc)

    def mix(r0, nr, t0, n):
        r, t = slice(r0, r0 + nr), slice(t0, t0 + n)
        obuf[r, t] = lax.dot_general(
            wbuf[r, :], gbuf[t, :], (((1,), (1,)), ((), ())), preferred_element_type=F32
        ).astype(BF16)

    def sums(r0, nr, t0, n):
        r, t = slice(r0, r0 + nr), slice(t0, t0 + n)
        for cc in range(2):
            c = slice(cc * quarter, (cc + 1) * quarter)
            gw = jnp.dot(abuf[r, t], gbuf[t, c], preferred_element_type=F32)
            for piece in range(nr // rows):
                p = slice(piece * rows, (piece + 1) * rows)
                g = gw[p]
                w = wbuf[r0 + piece * rows:r0 + (piece + 1) * rows, c].astype(F32)
                slot, l_at = (r0 // rows + piece) // NL, piece % NL
                at_row = cc * 4 + l_at
                lacc[slot, at_row:at_row + 1, :] += jnp.sum(g * w, axis=0, keepdims=True)
                lacc[slot, at_row + 2:at_row + 3, :] += jnp.sum(g, axis=0, keepdims=True)

    def compute(r0, nr, t0, n):
        mix(r0, nr, t0, n)
        sums(r0, nr, t0, n)

    def z_at(slot):
        return (z + Z_OFF[slot]) % NZ

    early = (NX - 1) * tokens
    lanes = (slice(0, nt), slice(nt, nt + early), slice(nt + early, 2 * nt))
    into = (slice(0, nt), slice(0, early), slice(early, nt))

    def tile(buf, slot, part):
        return buf.at[slot * chunk:(slot + 1) * chunk, lanes[part]]

    def slot_of(z_to):
        off = (z_to - z + NZ) % NZ
        return jnp.where(off == 0, 0, jnp.where(off < 4, 2 * off - 1, jnp.where(off == 4, 7, 2 * (NZ - off))))

    def ycopy(src, dst_at, part, zp, device):
        dst = yrecv.at[dst_at, zp, :, into[part]]
        return copy(src, dst, os_.at[0], or_.at[(dst_at * 3 + part) * 2 + zp], device)

    def block(buf, slot):
        return buf.at[pl.ds(pl.multiple_of(slot * chunk, chunk), chunk), lanes[2]]

    def last_send():
        for n in range(4):
            slot = slot_of(n // 2 * 4 + 2 * (1 - k) + n % 2)
            copy(block(obuf, slot), block(krecv, slot), ks.at[0], kr.at[slot * 3 + 2], core).start()

    def last_drain():
        for n in range(4):
            slot = slot_of(n // 2 * 4 + 2 * k + n % 2)
            arrived(block(krecv, slot), ks.at[0], kr.at[slot * 3 + 2])
            total = block(obuf, slot)[...].astype(F32) + block(krecv, slot)[...].astype(F32)
            block(ybuf, slot)[...] = total.astype(BF16)
            ycopy(block(ybuf, slot), jnp.where(h == n // 2, 1, 2), 2, n % 2, at(l_=1 - l, h_=n // 2)).start()

    def ksend(slots, parts):
        for slot in slots:
            for part in parts:
                i = slot * 3 + part

                @pl.when((z_at(slot) // 2) % 2 != k)
                def _():
                    copy(tile(obuf, slot, part), tile(krecv, slot, part), ks.at[0], kr.at[i], core).start()

    def kdrain_one(slot, part):
        i = slot * 3 + part
        zz = z_at(slot)

        @pl.when((zz // 2) % 2 == k)
        def _():
            arrived(tile(krecv, slot, part), ks.at[0], kr.at[i])
            total = tile(obuf, slot, part)[...].astype(F32) + tile(krecv, slot, part)[...].astype(F32)
            tile(ybuf, slot, part)[...] = total.astype(BF16)
            zp = zz % 2
            src = tile(ybuf, slot, part)
            if part == 0:
                @pl.when(zz // 4 != h)
                def _():
                    ycopy(src, 0, part, zp, across).start()
            else:
                ycopy(src, jnp.where(zz // 4 == h, 1, 2), part, zp, at(l_=1 - l, h_=zz // 4)).start()

    def kdrain(slots, parts):
        for slot in slots:
            for part in parts:
                kdrain_one(slot, part)

    eighth = quarter // 2

    def folded(slot):
        return jnp.concatenate([lacc[slot, :, 0:eighth], lacc[slot, :, eighth:quarter]], axis=0)

    def lsend(slot):
        lsent[slot - 1, :, 0:eighth] = folded(slot).astype(BF16)
        send(lsent.at[slot - 1], lrecv.at[Z_INV[slot] - 1], ls.at[0], lr.at[Z_INV[slot] - 1], zs_of[slot])

    t1, t2, t3, t4 = 3 * tokens, 2 * tokens, 2 * tokens, tokens
    zpass(1, 0)
    send(go_ref.at[:, other_cols], grows(0, 1), ys.at[0], yr.at[1], direct)
    arrived(wrows(0, 1), ys.at[0], yr.at[0])
    zpass(0, 1)
    for j in range(1, NX):
        arrived(ablock(j * tokens, tokens), as_.at[0], ar.at[j - 1])
    send(ablock(0, nt), ablock(0, nt), as_.at[0], ar.at[3], core)
    send(ablock(0, nt), ablock(nt, nt), as_.at[0], ar.at[4], wrap)
    zpass(2, 0)
    xpass(0)
    zpass(1, 1)
    loads[5].wait()
    arrived(grows(0, 1), ys.at[0], yr.at[1])
    xown(1)
    xwait(1, 0)
    other_half = pl.multiple_of((1 - k) * hrows, hrows)
    arrived(ablock(0, nt, other_half), as_.at[0], ar.at[3])
    compute(0, 3 * chunk, 0, t1)
    zpass(3, 0)
    arrived(ablock(nt, nt), as_.at[0], ar.at[4])
    send(ablock(nt, nt), ablock(nt, nt), as_.at[0], ar.at[5], core)
    zpass(2, 1)
    xwait(2, 0)
    arrived(ablock(nt, nt, other_half), as_.at[0], ar.at[5])
    compute(0, 3 * chunk, t1, t2)
    ksend((0, 1, 2), (0,))
    xpass(1)
    compute(3 * chunk, 2 * chunk, 0, t1 + t2)
    ksend((3, 4), (0,))
    kdrain((0, 1, 2), (0,))
    zpass(3, 1)
    xwait(1, 1)
    compute(0, 5 * chunk, t1 + t2, t3)
    ksend((0, 1, 2, 3, 4), (1,))
    kdrain((3, 4), (0,))
    compute(5 * chunk, 2 * chunk, 0, t1 + t2 + t3)
    ksend((5, 6), (0, 1))
    kdrain((0, 1, 2, 3, 4), (1,))
    xwait(2, 1)
    mix(0, 7 * chunk, t1 + t2 + t3, t4)
    sums(0, 7 * chunk, t1 + t2 + t3, t4)
    for s in range(1, 7):
        lsend(s)
    kdrain((5, 6), (0, 1))
    zlast(0)
    zlast(1)
    sums(7 * chunk, chunk, 0, 2 * nt)
    lsend(7)
    mix(7 * chunk, chunk, 0, 2 * nt)
    ksend((7,), (0, 1))
    last_send()
    kdrain((7,), (0, 1))
    last_drain()

    total = folded(0)
    for s in range(1, NZ):
        arrived(lrecv.at[s - 1], ls.at[0], lr.at[s - 1])
        total += lrecv[s - 1, :, 0:eighth].astype(F32)
    factors = []
    for side in range(2):
        for cc in range(2):
            columns = pl.ds(pl.multiple_of(l * half + cc * quarter, 128), quarter)
            factors.append(jnp.ones((2, eighth), F32))
            for l_at in range(NL):
                scale = scale32[pl.ds((z * NL + l_at) * 2 + x // 2 - base, 1), columns]
                factors.append(-scale[:, side * eighth:(side + 1) * eighth])
    total *= jnp.concatenate(factors, axis=0)
    width = log_ref.shape[1]
    for j in range(fsend.shape[0]):
        cc, m = j // (quarter // width), j % (quarter // width)
        side, m = m // (eighth // width), m % (eighth // width)
        fsend[j, :, 0:width] = total[side * 8 + cc * 4:side * 8 + cc * 4 + 4, m * width:(m + 1) * width]
    here = z * NX + x
    for n in range(lows * NL * NX):
        zq, l_to, x_to = (z + n // (NL * NX)) % lows, (l + n // NX) % NL, (x + n) % NX
        src, dst = fsend.at[(zq * NL + l_to) * NX + x_to], frecv.at[here]
        device = at(z_=l * lows + zq, l_=l_to, x_=x_to)
        if n:
            copy(src, dst, es.at[0], er.at[0], device).start()
        else:
            @pl.when(jnp.logical_not(is_mine))
            def _():
                copy(src, dst, es.at[0], er.at[0], device).start()

            @pl.when(is_mine)
            def _():
                pltpu.make_async_copy(src, dst, er.at[0]).start()

    q = h * NK + k
    for part in (1, 2):
        for zp in range(2):
            slot = slot_of(2 * q + zp)
            if part == 1:
                arrived(yrecv.at[0, zp], os_.at[0], or_.at[zp])
            for src in (1, 2):
                arrived(yrecv.at[src, zp, :, into[part]], os_.at[0], or_.at[(src * 3 + part) * 2 + zp])
            total = ybuf[pl.ds(pl.multiple_of(slot * chunk, chunk), chunk), into[part]].astype(F32)
            for src in range(3):
                total += yrecv[src, zp, :, into[part]].astype(F32)
            yown[zp, :, into[part]] = total.astype(BF16)
            for j in (1, 2) if part == 1 else (3,):
                i = (j - 1) * 2 + zp
                r = (X_INV[j] - 1) * 2 + zp
                send(yown.at[zp, :, j * tokens:(j + 1) * tokens], xrecv.at[X_INV[j] - 1, zp], fs.at[0], fr.at[r], xs_of[j])

    for zp in range(2):
        for j in range(NX):
            if j:
                arrived(xrecv.at[j - 1, zp], fs.at[0], fr.at[(j - 1) * 2 + zp])
            x_at = (x + X_OFF[j]) % NX
            for l_at in range(NL):
                p = slice(l_at * rows, (l_at + 1) * rows)
                piece = xrecv[j - 1, zp, p, :] if j else yown[zp, p, 0:tokens]
                first = ((zp * NL + l_at) * NX + x_at) * rows
                fin[pl.ds(pl.multiple_of(first, rows), rows), :] = piece
    for c in range(0, fin.shape[0], 128):
        out_ref[:, c:c + 128] = fin[c:c + 128, :].T

    copy(frecv, frecv, es.at[0], er.at[0], core).wait_recv()
    for zj in range(NZ):
        for pair in range(NX // 2):
            four = frecv[zj * NX + 2 * pair] + frecv[zj * NX + 2 * pair + 1]
            for l_at in range(NL):
                g = (zj * NL + l_at) * 2 + pair
                log_ref[g:g + 1, :] = four[l_at:l_at + 1, 0:width]
                zero_ref[g:g + 1, :] = four[2 + l_at:3 + l_at, 0:width]

    all_sent(wbuf.at[0:7 * chunk, :], zs.at[0])
    all_sent(gbuf.at[0:6 * tokens, :], xs.at[0])
    all_sent(wsend, ys.at[0])
    all_sent(grows(0, 0), ys.at[0])
    all_sent(asend, as_.at[0])
    for _ in range(3):
        all_sent(ablock(0, nt), as_.at[0])
    all_sent(obuf.at[0:4 * chunk, :], ks.at[0])
    all_sent(ybuf.at[0:3 * chunk, :], os_.at[0])
    all_sent(xrecv, fs.at[0])
    all_sent(lsent, ls.at[0])
    copy(frecv.at[0:NZ * NX - 1], frecv.at[0:NZ * NX - 1], es.at[0], er.at[0], core).wait_send()

    @pl.when(jnp.logical_not(is_mine))
    def _():
        copy(frecv.at[0], frecv.at[0], es.at[0], er.at[0], core).wait_send()


def on_device(activations, grad_out, weight_codes, scales, zero_points):
    tokens, features = activations.shape
    rows, cols = weight_codes.shape
    half = cols // NL
    groups = scales.shape[0]
    chunk, nt = NL * rows, NX * tokens
    vmem = pl.BlockSpec(memory_space=pltpu.VMEM)
    dma = pltpu.SemaphoreType.DMA
    width = cols // (NZ * NL * NX)
    hbm = pl.BlockSpec(memory_space=pltpu.HBM)
    out, log_sums, zero_sums = pl.pallas_call(
        kernel,
        out_shape=(
            jax.ShapeDtypeStruct((tokens, features // (NH * NK)), BF16),
            jax.ShapeDtypeStruct((groups, width), F32),
            jax.ShapeDtypeStruct((groups, width), F32),
        ),
        in_specs=[hbm] * 5,
        out_specs=(vmem, vmem, vmem),
        scratch_shapes=[
            pltpu.VMEM((tokens, features), BF16),
            pltpu.VMEM((2, rows, half), jnp.int32),
            pltpu.VMEM((16, cols), BF16),
            pltpu.VMEM((16, cols), jnp.int32),
            pltpu.VMEM((16, cols), F32),
            pltpu.VMEM((half // width, 4, 128), F32),
            pltpu.VMEM((NZ * NX, 4, 128), F32),
            pltpu.VMEM((NZ * chunk, half), BF16),
            pltpu.VMEM((rows, half), BF16),
            pltpu.VMEM((NL * nt, half), BF16),
            pltpu.VMEM((features, tokens), BF16),
            pltpu.VMEM((NX - 1, NZ // 2 * chunk, tokens), BF16),
            pltpu.VMEM((NZ * chunk, NL * nt), BF16),
            pltpu.VMEM((NZ * chunk, NL * nt), BF16),
            pltpu.VMEM((NZ * chunk, NL * nt), BF16),
            pltpu.VMEM((NZ * chunk, NL * nt), BF16),
            pltpu.VMEM((3, 2, chunk, nt), BF16),
            pltpu.VMEM((2, chunk, nt), BF16),
            pltpu.VMEM((NX - 1, 2, chunk, tokens), BF16),
            pltpu.VMEM((2 * NX * chunk, tokens), BF16),
            pltpu.VMEM((NZ, 8, half // 2), F32),
            pltpu.VMEM((NZ - 1, 16, 512), BF16),
            pltpu.VMEM((NZ - 1, 16, 512), BF16),
            dma((6,)),
            dma((1,)), dma((32,)),
            dma((1,)), dma((12,)),
            dma((1,)), dma((2,)),
            dma((1,)), dma((6,)),
            dma((1,)), dma((24,)),
            dma((1,)), dma((18,)),
            dma((1,)), dma((6,)),
            dma((1,)), dma((7,)),
            dma((1,)), dma((1,)),
        ],
        compiler_params=pltpu.CompilerParams(
            collective_id=0, has_side_effects=True, vmem_limit_bytes=63 * 2**20
        ),
        cost_estimate=pl.CostEstimate(
            flops=4 * NZ * chunk * NL * nt * half, bytes_accessed=4 * 2**20, transcendentals=0
        ),
    )(activations, grad_out, weight_codes, scales, zero_points)

    return (out, log_sums[:, None, :], zero_sums[:, None, :])


def solution(mesh):
    in_specs = (
        P("dp", None),
        P("dp", "tensor"),
        P("dp", "tensor"),
        P(None, "tensor"),
        P(None, "tensor"),
    )
    out_specs = (P("dp", "tensor"), P(None, "tensor", "dp"), P(None, "tensor", "dp"))
    return jax.shard_map(
        on_device, mesh=mesh, in_specs=in_specs, out_specs=out_specs, check_vma=False
    )
```

```python
import jax
import jax.numpy as jnp
from jax import lax
from jax.experimental import pallas as pl
from jax.experimental.pallas import tpu as pltpu
from jax.sharding import PartitionSpec as P

NZ, NL, NX, NH, NK = 8, 2, 4, 2, 2
MESH = pl.DeviceIdType.MESH
F32, BF16 = jnp.float32, jnp.bfloat16
Z_OFF = (0, 1, 7, 2, 6, 3, 5, 4)
Z_INV = (0, 2, 1, 4, 3, 6, 5, 7)
X_OFF = (0, 1, 3, 2)
X_INV = (0, 2, 1, 3)


def kernel(
    act_ref, go_ref, codes_ref, scales_ref, zeros_ref,
    out_ref, log_ref, zero_ref,
    act_v, codes_v, scales_v, zeros_v, scale32, fsend, frecv, wbuf, wsend, gbuf, act_t, asend, abuf, obuf, krecv, ybuf, yrecv, yown, xrecv,
    fin, lacc, lsent, lrecv,
    ins, zs, zr, xs, xr, ys, yr, as_, ar, ks, kr, os_, or_, fs, fr, ls, lr, es, er,
):
    dp, tensor = lax.axis_index("dp"), lax.axis_index("tensor")
    z, l, x = dp // (NL * NX), (dp // NX) % NL, dp % NX
    h, k = tensor // NK, tensor % NK
    rows, cols = codes_ref.shape
    tokens = go_ref.shape[0]
    half = cols // NL
    chunk = NL * rows
    nt = NX * tokens
    quarter = lacc.shape[2]

    def at(z_=z, l_=l, x_=x, h_=h, k_=k):
        return ((z_ * NL + l_) * NX + x_, h_ * NK + k_)

    direct = at(l_=1 - l)
    wrap = at(l_=1 - l, h_=1 - h)
    across = at(h_=1 - h)
    core = at(k_=1 - k)
    xs_of = [at(x_=(x + o) % NX) for o in X_OFF]
    zs_of = [at(z_=(z + o) % NZ) for o in Z_OFF]

    def copy(src, dst, send, recv, device):
        return pltpu.make_async_remote_copy(
            src_ref=src, dst_ref=dst, send_sem=send, recv_sem=recv,
            device_id=device, device_id_type=MESH,
        )

    def send(src, dst, s, r, device):
        copy(src, dst, s, r, device).start()

    def all_sent(ref, s):
        copy(ref, ref, s, s, core).wait_send()

    def arrived(dst, s, r):
        copy(dst, dst, s, r, core).wait_recv()

    own_cols = pl.ds(pl.multiple_of(l * half, 128), half)
    other_cols = pl.ds(pl.multiple_of((1 - l) * half, 128), half)
    group = dp // 2
    base = pl.multiple_of(group // 16 * 16, 16)
    barrier = pltpu.get_barrier_semaphore()
    loads = [
        pltpu.make_async_copy(src, dst, ins.at[i])
        for i, (src, dst) in enumerate((
            (scales_ref.at[pl.ds(base, 16), :], scales_v),
            (zeros_ref.at[pl.ds(base, 16), :], zeros_v),
            (codes_ref.at[:, other_cols], codes_v.at[1]),
            (codes_ref.at[:, own_cols], codes_v.at[0]),
            (act_ref, act_v),
            (go_ref.at[:, own_cols], gbuf.at[0:tokens, :]),
        ))
    ]
    for load in loads:
        load.start()
    partners = zs_of[1:3] + xs_of[1:] + [direct, wrap, core]
    for device in partners:
        pl.semaphore_signal(barrier, inc=1, device_id=device, device_id_type=MESH)
    lows = NZ // NL
    is_mine = z // lows == l
    part_rows = (
        pl.multiple_of(l * rows, rows),
        pl.multiple_of((1 - l) * rows, rows),
    )
    loads[0].wait()
    loads[1].wait()
    scale32[...] = scales_v[...].astype(F32)

    def dequantized(side, columns):
        scale = scale32[pl.ds(group - base, 1), columns]
        zero = zeros_v[pl.ds(group - base, 1), columns]
        return (scale * (codes_v[side] - zero).astype(F32)).astype(BF16)

    loads[2].wait()
    wsend[...] = dequantized(1, other_cols)
    loads[3].wait()
    wbuf[pl.ds(part_rows[0], rows), :] = dequantized(0, own_cols)
    features = act_ref.shape[1]
    loads[4].wait()
    for c in range(0, features, 128):
        act_t[c:c + 128, :] = act_v[:, c:c + 128].T
    hrows = NZ // 2 * chunk
    my_half = pl.multiple_of(k * hrows, hrows)
    for i in range(NZ // 2):
        z_at = (z + jnp.where(k == 0, Z_OFF[i], Z_OFF[NZ // 2 + i])) % NZ
        for l_at in range(NL):
            for j in range(NX):
                first = pl.multiple_of(((z_at * NL + l_at) * NX + (x + X_OFF[j]) % NX) * rows, rows)
                piece = act_t[pl.ds(first, rows), :]
                place = i * chunk + l_at * rows
                if j:
                    asend[j - 1, place:place + rows, :] = piece
                else:
                    abuf[pl.ds(pl.multiple_of(my_half + place, rows), rows), 0:tokens] = piece

    pl.semaphore_wait(barrier, len(partners))

    def wrows(slot, part, sub=None):
        count = rows if sub is None else rows // 2
        return wbuf.at[pl.ds(slot * chunk + part_rows[part] + (sub or 0) * (rows // 2), count), :]

    def zcopy(step, part, sub, way):
        src = wrows(2 * step - way if step else 0, part, sub)
        dst = wrows(2 * (step + 1) - way if step < 3 else 7, part, sub)
        i = ((way * 4 + step) * 2 + part) * 2 + sub
        return src, dst, zs.at[0], zr.at[i], zs_of[1 + way]

    def zpass(step, part):
        for n in range(2):
            for way in range(2):
                sub = n if way == 0 else 1 - n
                if step:
                    arrived(*zcopy(step - 1, part, sub, way)[1:4])
                if step < 3 or n == 0:
                    send(*zcopy(step, part, sub, way))

    def zlast(part):
        for way in range(2):
            arrived(*zcopy(3, part, way, way)[1:4])

    def grows(slot, part, first=0, count=None):
        start = part * nt + slot * tokens + first
        return gbuf.at[start:start + (count or tokens), :]

    turn = tokens // 2

    def xcopy(kind, part, way):
        first, count = (0, turn) if (kind == 1) == (way == 1) else (turn, tokens - turn)
        if kind == 2:
            src, dst = grows(2 - way, part, first, count), grows(3, part, first, count)
        else:
            src = grows(0, 1, first, count) if part else go_ref.at[first:first + count, own_cols]
            dst = grows(2 - way, part, first, count)
        i = (way * 3 + kind) * 2 + part
        return src, dst, xs.at[0], xr.at[i], xs_of[1 + way]

    def xown(part):
        for kind in (0, 1):
            for way in range(2):
                send(*xcopy(kind, part, way))

    def xpass(part):
        for way in range(2):
            arrived(*xcopy(0, part, way)[1:4])
            send(*xcopy(2, part, way))

    def xwait(kind, part):
        for way in range(2):
            arrived(*xcopy(kind, part, way)[1:4])

    def ablock(first, count, half_at=None):
        start = my_half if half_at is None else half_at
        return abuf.at[pl.ds(start, hrows), first:first + count]

    send(wsend, wrows(0, 0), ys.at[0], yr.at[0], direct)
    zpass(0, 0)
    for j in range(1, NX):
        send(asend.at[j - 1], ablock(X_INV[j] * tokens, tokens), as_.at[0], ar.at[X_INV[j] - 1], xs_of[j])
    xown(0)

    lacc[...] = jnp.zeros_like(lacc)

    def mix(r0, nr, t0, n):
        r, t = slice(r0, r0 + nr), slice(t0, t0 + n)
        obuf[r, t] = lax.dot_general(
            wbuf[r, :], gbuf[t, :], (((1,), (1,)), ((), ())), preferred_element_type=F32
        ).astype(BF16)

    def sums(r0, nr, t0, n):
        r, t = slice(r0, r0 + nr), slice(t0, t0 + n)
        for cc in range(2):
            c = slice(cc * quarter, (cc + 1) * quarter)
            gw = jnp.dot(abuf[r, t], gbuf[t, c], preferred_element_type=F32)
            for piece in range(nr // rows):
                p = slice(piece * rows, (piece + 1) * rows)
                g = gw[p]
                w = wbuf[r0 + piece * rows:r0 + (piece + 1) * rows, c].astype(F32)
                slot, l_at = (r0 // rows + piece) // NL, piece % NL
                at_row = cc * 4 + l_at
                lacc[slot, at_row:at_row + 1, :] += jnp.sum(g * w, axis=0, keepdims=True)
                lacc[slot, at_row + 2:at_row + 3, :] += jnp.sum(g, axis=0, keepdims=True)

    def compute(r0, nr, t0, n):
        mix(r0, nr, t0, n)
        sums(r0, nr, t0, n)

    def z_at(slot):
        return (z + Z_OFF[slot]) % NZ

    early = (NX - 1) * tokens
    lanes = (slice(0, nt), slice(nt, nt + early), slice(nt + early, 2 * nt))
    into = (slice(0, nt), slice(0, early), slice(early, nt))

    def tile(buf, slot, part):
        return buf.at[slot * chunk:(slot + 1) * chunk, lanes[part]]

    def slot_of(z_to):
        off = (z_to - z + NZ) % NZ
        return jnp.where(off == 0, 0, jnp.where(off < 4, 2 * off - 1, jnp.where(off == 4, 7, 2 * (NZ - off))))

    def ycopy(src, dst_at, part, zp, device):
        dst = yrecv.at[dst_at, zp, :, into[part]]
        return copy(src, dst, os_.at[0], or_.at[(dst_at * 3 + part) * 2 + zp], device)

    def block(buf, slot):
        return buf.at[pl.ds(pl.multiple_of(slot * chunk, chunk), chunk), lanes[2]]

    def last_send():
        for n in range(4):
            slot = slot_of(n // 2 * 4 + 2 * (1 - k) + n % 2)
            copy(block(obuf, slot), block(krecv, slot), ks.at[0], kr.at[slot * 3 + 2], core).start()

    def last_drain():
        for n in range(4):
            slot = slot_of(n // 2 * 4 + 2 * k + n % 2)
            arrived(block(krecv, slot), ks.at[0], kr.at[slot * 3 + 2])
            total = block(obuf, slot)[...].astype(F32) + block(krecv, slot)[...].astype(F32)
            block(ybuf, slot)[...] = total.astype(BF16)
            ycopy(block(ybuf, slot), jnp.where(h == n // 2, 1, 2), 2, n % 2, at(l_=1 - l, h_=n // 2)).start()

    def ksend(slots, parts):
        for slot in slots:
            for part in parts:
                i = slot * 3 + part

                @pl.when((z_at(slot) // 2) % 2 != k)
                def _():
                    copy(tile(obuf, slot, part), tile(krecv, slot, part), ks.at[0], kr.at[i], core).start()

    def kdrain_one(slot, part):
        i = slot * 3 + part
        zz = z_at(slot)

        @pl.when((zz // 2) % 2 == k)
        def _():
            arrived(tile(krecv, slot, part), ks.at[0], kr.at[i])
            total = tile(obuf, slot, part)[...].astype(F32) + tile(krecv, slot, part)[...].astype(F32)
            tile(ybuf, slot, part)[...] = total.astype(BF16)
            zp = zz % 2
            src = tile(ybuf, slot, part)
            if part == 0:
                @pl.when(zz // 4 != h)
                def _():
                    ycopy(src, 0, part, zp, across).start()
            else:
                ycopy(src, jnp.where(zz // 4 == h, 1, 2), part, zp, at(l_=1 - l, h_=zz // 4)).start()

    def kdrain(slots, parts):
        for slot in slots:
            for part in parts:
                kdrain_one(slot, part)

    eighth = quarter // 2

    def folded(slot):
        return jnp.concatenate([lacc[slot, :, 0:eighth], lacc[slot, :, eighth:quarter]], axis=0)

    def lsend(slot):
        lsent[slot - 1, :, 0:eighth] = folded(slot).astype(BF16)
        send(lsent.at[slot - 1], lrecv.at[Z_INV[slot] - 1], ls.at[0], lr.at[Z_INV[slot] - 1], zs_of[slot])

    t1, t2, t3, t4 = 3 * tokens, 2 * tokens, 2 * tokens, tokens
    zpass(1, 0)
    send(go_ref.at[:, other_cols], grows(0, 1), ys.at[0], yr.at[1], direct)
    arrived(wrows(0, 1), ys.at[0], yr.at[0])
    zpass(0, 1)
    for j in range(1, NX):
        arrived(ablock(j * tokens, tokens), as_.at[0], ar.at[j - 1])
    send(ablock(0, nt), ablock(0, nt), as_.at[0], ar.at[3], core)
    send(ablock(0, nt), ablock(nt, nt), as_.at[0], ar.at[4], wrap)
    zpass(2, 0)
    xpass(0)
    zpass(1, 1)
    loads[5].wait()
    arrived(grows(0, 1), ys.at[0], yr.at[1])
    xown(1)
    xwait(1, 0)
    other_half = pl.multiple_of((1 - k) * hrows, hrows)
    arrived(ablock(0, nt, other_half), as_.at[0], ar.at[3])
    compute(0, 3 * chunk, 0, t1)
    zpass(3, 0)
    arrived(ablock(nt, nt), as_.at[0], ar.at[4])
    send(ablock(nt, nt), ablock(nt, nt), as_.at[0], ar.at[5], core)
    zpass(2, 1)
    xwait(2, 0)
    arrived(ablock(nt, nt, other_half), as_.at[0], ar.at[5])
    compute(0, 3 * chunk, t1, t2)
    ksend((0, 1, 2), (0,))
    xpass(1)
    compute(3 * chunk, 2 * chunk, 0, t1 + t2)
    ksend((3, 4), (0,))
    kdrain((0, 1, 2), (0,))
    zpass(3, 1)
    xwait(1, 1)
    compute(0, 5 * chunk, t1 + t2, t3)
    ksend((0, 1, 2, 3, 4), (1,))
    kdrain((3, 4), (0,))
    compute(5 * chunk, 2 * chunk, 0, t1 + t2 + t3)
    ksend((5, 6), (0, 1))
    kdrain((0, 1, 2, 3, 4), (1,))
    xwait(2, 1)
    mix(0, 7 * chunk, t1 + t2 + t3, t4)
    sums(0, 7 * chunk, t1 + t2 + t3, t4)
    for s in range(1, 7):
        lsend(s)
    kdrain((5, 6), (0, 1))
    zlast(0)
    zlast(1)
    sums(7 * chunk, chunk, 0, 2 * nt)
    lsend(7)
    mix(7 * chunk, chunk, 0, 2 * nt)
    ksend((7,), (0, 1))
    last_send()
    kdrain((7,), (0, 1))
    last_drain()

    total = folded(0)
    for s in range(1, NZ):
        arrived(lrecv.at[s - 1], ls.at[0], lr.at[s - 1])
        total += lrecv[s - 1, :, 0:eighth].astype(F32)
    factors = []
    for side in range(2):
        for cc in range(2):
            columns = pl.ds(pl.multiple_of(l * half + cc * quarter, 128), quarter)
            factors.append(jnp.ones((2, eighth), F32))
            for l_at in range(NL):
                scale = scale32[pl.ds((z * NL + l_at) * 2 + x // 2 - base, 1), columns]
                factors.append(-scale[:, side * eighth:(side + 1) * eighth])
    total *= jnp.concatenate(factors, axis=0)
    width = log_ref.shape[1]
    for j in range(fsend.shape[0]):
        cc, m = j // (quarter // width), j % (quarter // width)
        side, m = m // (eighth // width), m % (eighth // width)
        fsend[j, :, 0:width] = total[side * 8 + cc * 4:side * 8 + cc * 4 + 4, m * width:(m + 1) * width]
    here = z * NX + x
    for n in range(lows * NL * NX):
        zq, l_to, x_to = (z + n // (NL * NX)) % lows, (l + n // NX) % NL, (x + n) % NX
        src, dst = fsend.at[(zq * NL + l_to) * NX + x_to], frecv.at[here]
        device = at(z_=l * lows + zq, l_=l_to, x_=x_to)
        if n:
            copy(src, dst, es.at[0], er.at[0], device).start()
        else:
            @pl.when(jnp.logical_not(is_mine))
            def _():
                copy(src, dst, es.at[0], er.at[0], device).start()

            @pl.when(is_mine)
            def _():
                pltpu.make_async_copy(src, dst, er.at[0]).start()

    q = h * NK + k
    for part in (1, 2):
        for zp in range(2):
            slot = slot_of(2 * q + zp)
            if part == 1:
                arrived(yrecv.at[0, zp], os_.at[0], or_.at[zp])
            for src in (1, 2):
                arrived(yrecv.at[src, zp, :, into[part]], os_.at[0], or_.at[(src * 3 + part) * 2 + zp])
            total = ybuf[pl.ds(pl.multiple_of(slot * chunk, chunk), chunk), into[part]].astype(F32)
            for src in range(3):
                total += yrecv[src, zp, :, into[part]].astype(F32)
            yown[zp, :, into[part]] = total.astype(BF16)
            for j in (1, 2) if part == 1 else (3,):
                i = (j - 1) * 2 + zp
                r = (X_INV[j] - 1) * 2 + zp
                send(yown.at[zp, :, j * tokens:(j + 1) * tokens], xrecv.at[X_INV[j] - 1, zp], fs.at[0], fr.at[r], xs_of[j])

    for zp in range(2):
        for j in range(NX):
            if j:
                arrived(xrecv.at[j - 1, zp], fs.at[0], fr.at[(j - 1) * 2 + zp])
            x_at = (x + X_OFF[j]) % NX
            for l_at in range(NL):
                p = slice(l_at * rows, (l_at + 1) * rows)
                piece = xrecv[j - 1, zp, p, :] if j else yown[zp, p, 0:tokens]
                first = ((zp * NL + l_at) * NX + x_at) * rows
                fin[pl.ds(pl.multiple_of(first, rows), rows), :] = piece
    for c in range(0, fin.shape[0], 128):
        out_ref[:, c:c + 128] = fin[c:c + 128, :].T

    copy(frecv, frecv, es.at[0], er.at[0], core).wait_recv()
    for zj in range(NZ):
        for pair in range(NX // 2):
            four = frecv[zj * NX + 2 * pair] + frecv[zj * NX + 2 * pair + 1]
            for l_at in range(NL):
                g = (zj * NL + l_at) * 2 + pair
                log_ref[g:g + 1, :] = four[l_at:l_at + 1, 0:width]
                zero_ref[g:g + 1, :] = four[2 + l_at:3 + l_at, 0:width]

    all_sent(wbuf.at[0:7 * chunk, :], zs.at[0])
    all_sent(gbuf.at[0:6 * tokens, :], xs.at[0])
    all_sent(wsend, ys.at[0])
    all_sent(grows(0, 0), ys.at[0])
    all_sent(asend, as_.at[0])
    for _ in range(3):
        all_sent(ablock(0, nt), as_.at[0])
    all_sent(obuf.at[0:4 * chunk, :], ks.at[0])
    all_sent(ybuf.at[0:3 * chunk, :], os_.at[0])
    all_sent(xrecv, fs.at[0])
    all_sent(lsent, ls.at[0])
    copy(frecv.at[0:NZ * NX - 1], frecv.at[0:NZ * NX - 1], es.at[0], er.at[0], core).wait_send()

    @pl.when(jnp.logical_not(is_mine))
    def _():
        copy(frecv.at[0], frecv.at[0], es.at[0], er.at[0], core).wait_send()


def on_device(activations, grad_out, weight_codes, scales, zero_points):
    tokens, features = activations.shape
    rows, cols = weight_codes.shape
    half = cols // NL
    groups = scales.shape[0]
    chunk, nt = NL * rows, NX * tokens
    vmem = pl.BlockSpec(memory_space=pltpu.VMEM)
    dma = pltpu.SemaphoreType.DMA
    width = cols // (NZ * NL * NX)
    hbm = pl.BlockSpec(memory_space=pltpu.HBM)
    out, log_sums, zero_sums = pl.pallas_call(
        kernel,
        out_shape=(
            jax.ShapeDtypeStruct((tokens, features // (NH * NK)), BF16),
            jax.ShapeDtypeStruct((groups, width), F32),
            jax.ShapeDtypeStruct((groups, width), F32),
        ),
        in_specs=[hbm] * 5,
        out_specs=(vmem, vmem, vmem),
        scratch_shapes=[
            pltpu.VMEM((tokens, features), BF16),
            pltpu.VMEM((2, rows, half), jnp.int32),
            pltpu.VMEM((16, cols), BF16),
            pltpu.VMEM((16, cols), jnp.int32),
            pltpu.VMEM((16, cols), F32),
            pltpu.VMEM((half // width, 4, 128), F32),
            pltpu.VMEM((NZ * NX, 4, 128), F32),
            pltpu.VMEM((NZ * chunk, half), BF16),
            pltpu.VMEM((rows, half), BF16),
            pltpu.VMEM((NL * nt, half), BF16),
            pltpu.VMEM((features, tokens), BF16),
            pltpu.VMEM((NX - 1, NZ // 2 * chunk, tokens), BF16),
            pltpu.VMEM((NZ * chunk, NL * nt), BF16),
            pltpu.VMEM((NZ * chunk, NL * nt), BF16),
            pltpu.VMEM((NZ * chunk, NL * nt), BF16),
            pltpu.VMEM((NZ * chunk, NL * nt), BF16),
            pltpu.VMEM((3, 2, chunk, nt), BF16),
            pltpu.VMEM((2, chunk, nt), BF16),
            pltpu.VMEM((NX - 1, 2, chunk, tokens), BF16),
            pltpu.VMEM((2 * NX * chunk, tokens), BF16),
            pltpu.VMEM((NZ, 8, half // 2), F32),
            pltpu.VMEM((NZ - 1, 16, 512), BF16),
            pltpu.VMEM((NZ - 1, 16, 512), BF16),
            dma((6,)),
            dma((1,)), dma((32,)),
            dma((1,)), dma((12,)),
            dma((1,)), dma((2,)),
            dma((1,)), dma((6,)),
            dma((1,)), dma((24,)),
            dma((1,)), dma((18,)),
            dma((1,)), dma((6,)),
            dma((1,)), dma((7,)),
            dma((1,)), dma((1,)),
        ],
        compiler_params=pltpu.CompilerParams(
            collective_id=0, has_side_effects=True, vmem_limit_bytes=63 * 2**20
        ),
        cost_estimate=pl.CostEstimate(
            flops=4 * NZ * chunk * NL * nt * half, bytes_accessed=4 * 2**20, transcendentals=0
        ),
    )(activations, grad_out, weight_codes, scales, zero_points)

    return (out, log_sums[:, None, :], zero_sums[:, None, :])


def solution(mesh):
    in_specs = (
        P("dp", None),
        P("dp", "tensor"),
        P("dp", "tensor"),
        P(None, "tensor"),
        P(None, "tensor"),
    )
    out_specs = (P("dp", "tensor"), P(None, "tensor", "dp"), P(None, "tensor", "dp"))
    return jax.shard_map(
        on_device, mesh=mesh, in_specs=in_specs, out_specs=out_specs, check_vma=False
    )
```
